32 devices in a mesh: grp: 4 (over y, x), gx: 4 (over z), gy: 2 (over core).
Axes of the slice: x: 2, y: 2, z: 4, core: 2. Of those that a mesh axis runs over, the one named last changes fastest.
Arguments:
- modes_now: float32 [4, 32, 512, 1024], P('grp', ('gx', 'gy')), may hold values from -6 to 6
- modes_old: float32 [4, 32, 512, 1024], P('grp', ('gx', 'gy')), may hold values from -6 to 6
- pressure_now: float32 [4, 32, 512, 1024], P('grp', None, 'gx', 'gy'), may hold values from -6 to 6
- source: float32 [4, 32, 512, 1024], P('grp', None, 'gx', 'gy'), may hold values from -6 to 6
- strip_slot: int32 [4, 512, 2], P('grp', 'gx', 'gy'), may hold values from 0 to 127, as said below
- strip_row: int32 [4, 512, 2], P('grp', 'gx', 'gy'), may hold values from 0 to 127, as said below
Outputs:
- modes_new: float32 [4, 32, 512, 1024], P('grp', ('gx', 'gy'))
- pressure_next: float32 [4, 32, 512, 1024], P('grp', None, 'gx', 'gy')
The draws below stay inside these ranges and needn't reach their ends.
Inputs may be any that keep to these rules, and one draw needn't show every extreme that they name: The 128 strips of one device take distinct values of strip_slot. Each device sends to every other device (itself included) either no strip or exactly 4, and every bottom-face strip of every device is met by exactly one top-face strip. `strip_row`: see strip_slot.
All inputs are finite; a program needn't handle non-finite values.
Results may differ from the reference program's by a relative error of at most 0.00007.
Values sent between devices are 32-bit elements; how exact they have to be, the bound alone decides.
A program may use at most 128 MiB of HBM per device.

```python
import jax
import jax.numpy as jnp
from jax import lax

NXR = 512
NYR = 1024
NZ = 32
RECTS = 4
CX = 128
CY = 512
CAP = 4
N_GRP = 4
N_GX = 4
N_GY = 2
DEVICES = 32


def strip_plan(key):
    count = DEVICES
    per = CX
    slots_per = CAP
    groups = per // slots_per
    values = jnp.arange(count, dtype=jnp.int32)
    ranks = jax.random.permutation(jax.random.fold_in(key, 11), count).astype(jnp.int32)
    scores = jnp.where(values == count // 2, -2, jnp.where(values == count - 1, -1, ranks))
    offsets = jnp.argsort(scores, stable=True).astype(jnp.int32)[:groups]
    keys_send = jax.random.split(jax.random.fold_in(key, 12), count)
    order = jax.vmap(lambda one: jax.random.permutation(one, per))(keys_send).astype(jnp.int32)
    keys_recv = jax.random.split(jax.random.fold_in(key, 13), count)
    placing = jax.vmap(lambda one: jax.random.permutation(one, per))(keys_recv).astype(jnp.int32)
    sender = jnp.arange(count, dtype=jnp.int32)[:, None]
    position = jnp.arange(per, dtype=jnp.int32)[None, :]
    partner = (sender + offsets[position // slots_per]) % count
    slot_value = partner * slots_per + position % slots_per
    row_value = placing[partner, jnp.broadcast_to(position, partner.shape)]
    sender_full = jnp.broadcast_to(sender, partner.shape)
    slot_table = jnp.zeros((count, per), jnp.int32).at[sender_full, order].set(slot_value)
    row_table = jnp.zeros((count, per), jnp.int32).at[sender_full, order].set(row_value)
    return (slot_table, row_table)


def arrange(table):
    return table.reshape(N_GRP, N_GX, N_GY, CX).transpose(0, 1, 3, 2).reshape(N_GRP, NXR, N_GY)


def draw_strip_slot(key, part):
    slot_table, row_table = strip_plan(jax.random.fold_in(key, 5))
    return arrange(slot_table)


def draw_strip_row(key, part):
    slot_table, row_table = strip_plan(jax.random.fold_in(key, 5))
    return arrange(row_table)


def block_levels(stream_key, shape, pieces, low, high):
    def one(dim, blocks):
        draws = jax.random.uniform(jax.random.fold_in(jax.random.fold_in(stream_key, 6), dim), (blocks,), jnp.float32, low / len(pieces), high / len(pieces))
        return jnp.repeat(jnp.exp(draws), shape[dim] // blocks).reshape((-1,) + (1,) * (len(shape) - dim - 1))

    loudness = one(*pieces[0])
    for cut in pieces[1:]:
        loudness = loudness * one(*cut)
    return loudness


def scatter_about(stream_key, shape, width, reach, cuts=(), kind=jnp.bfloat16):
    result = width * jax.random.normal(stream_key, shape, jnp.float32)
    if cuts:
        result = result * block_levels(stream_key, shape, cuts, -0.22, 0.18)
    return jnp.clip(result, -reach, reach).astype(kind)


def setup_inputs(seed: int = 0) -> dict:
    key_list = jax.random.split(jax.random.key(seed), 7)
    return {
        "modes_now": scatter_about(key_list[0], (RECTS, NZ, NXR, NYR), 1.0, 6.0, ((0, 4), (1, 8)), jnp.float32),
        "modes_old": scatter_about(key_list[1], (RECTS, NZ, NXR, NYR), 1.0, 6.0, ((0, 4), (1, 8)), jnp.float32),
        "pressure_now": scatter_about(key_list[2], (RECTS, NZ, NXR, NYR), 1.0, 6.0, ((0, 4), (2, 4), (3, 2)), jnp.float32),
        "source": scatter_about(key_list[3], (RECTS, NZ, NXR, NYR), 1.0, 6.0, ((0, 4), (2, 4), (3, 2)), jnp.float32),
        "strip_slot": draw_strip_slot(jax.random.fold_in(key_list[6], 71), 0),
        "strip_row": draw_strip_row(jax.random.fold_in(key_list[6], 71), 0),
    }


COURANT = 0.5
WEIGHTS = (1.5, -0.15, 2.0 / 180.0)
HIGH = lax.Precision.HIGHEST

def cosine_table(count):
    rows = jnp.arange(count, dtype=jnp.int32).astype(jnp.float32)[:, None]
    cols = jnp.arange(count, dtype=jnp.int32).astype(jnp.float32)[None, :]
    scale = jnp.where(rows == 0, jnp.sqrt(1.0 / count), jnp.sqrt(2.0 / count))
    return (scale * jnp.cos(jnp.pi * rows * (cols + 0.5) / count)).astype(jnp.float32)

def face_stencil(diff):
    first = diff[..., 0, :]
    second = diff[..., 1, :]
    third = diff[..., 2, :]
    return jnp.stack([WEIGHTS[0] * first + WEIGHTS[1] * second + WEIGHTS[2] * third, WEIGHTS[1] * first + WEIGHTS[2] * second, WEIGHTS[2] * first], axis=-2)

def advance(current, previous, spectrum, depth_index, depth, long_x, long_y):
    index_x = jnp.arange(long_x, dtype=jnp.int32).astype(jnp.float32)
    index_y = jnp.arange(long_y, dtype=jnp.int32).astype(jnp.float32)
    part_z = depth_index / depth * (depth_index / depth)
    part_x = index_x / long_x * (index_x / long_x)
    part_y = index_y / long_y * (index_y / long_y)
    theta = COURANT * jnp.pi * jnp.sqrt(part_z[:, None, None] + part_x[None, :, None] + part_y[None, None, :])
    shape = jnp.sinc(theta / (2.0 * jnp.pi))
    return 2.0 * jnp.cos(theta) * current - previous + COURANT * COURANT * shape * shape * spectrum

def forward_field(field, table_z, table_x, table_y):
    part = jnp.einsum('kz,zxy->kxy', table_z, field, precision=HIGH)
    part = jnp.einsum('bx,kxy->kby', table_x, part, precision=HIGH)
    return jnp.einsum('cy,kby->kbc', table_y, part, precision=HIGH)

def inverse_field(modes, table_z, table_x, table_y):
    part = jnp.einsum('cy,abc->aby', table_y, modes, precision=HIGH)
    part = jnp.einsum('bx,aby->axy', table_x, part, precision=HIGH)
    return jnp.einsum('az,axy->zxy', table_z, part, precision=HIGH)

def to_strips(layers):
    return layers.reshape(RECTS, 3, NXR, N_GY, CY).transpose(0, 2, 3, 1, 4)

def from_strips(strips):
    return strips.transpose(0, 3, 1, 2, 4).reshape(RECTS, 3, NXR, NYR)

def reference(modes_now, modes_old, pressure_now, source, strip_slot, strip_row):
    table_z = cosine_table(NZ)
    table_x = cosine_table(NXR)
    table_y = cosine_table(NYR)
    pressure = pressure_now
    top_layers = jnp.stack([pressure[:, NZ - 1], pressure[:, NZ - 2], pressure[:, NZ - 3]], axis=1)
    top_strips = to_strips(top_layers)
    bottom_strips = to_strips(pressure[:, 0:3])
    partner = strip_slot // CAP
    group_p = partner // (N_GX * N_GY)
    block_x = partner // N_GY % N_GX
    block_y = partner % N_GY
    row_p = block_x * CX + strip_row
    met = bottom_strips[group_p, row_p, block_y]
    force = face_stencil(met - top_strips)
    bottom_force = jnp.zeros_like(bottom_strips).at[group_p, row_p, block_y].add(-force)
    bottom_field = from_strips(bottom_force)
    top_field = from_strips(force)
    forcing = source.at[:, 0:3].add(bottom_field)
    forcing = forcing.at[:, NZ - 1].add(top_field[:, 0])
    forcing = forcing.at[:, NZ - 2].add(top_field[:, 1])
    forcing = forcing.at[:, NZ - 3].add(top_field[:, 2])
    depth_index = jnp.arange(NZ, dtype=jnp.int32).astype(jnp.float32)

    def step_one(items):
        field, current, previous = items
        spectrum = forward_field(field, table_z, table_x, table_y)
        return advance(current, previous, spectrum, depth_index, NZ, NXR, NYR)
    modes_new = lax.map(step_one, (forcing, modes_now, modes_old))
    pressure_next = lax.map(lambda one: inverse_field(one, table_z, table_x, table_y), modes_new)
    return (modes_new, pressure_next)
```

```python
import functools

import jax
import jax.numpy as jnp
import ml_dtypes
import numpy as np
from jax import lax
from jax.experimental import pallas as pl
from jax.experimental.pallas import tpu as pltpu
from jax.sharding import PartitionSpec as P

COURANT = 0.5
WEIGHTS = (1.5, -0.15, 2.0 / 180.0)
HIGH = lax.Precision.HIGHEST


def cosine_table(count):
    rows = np.arange(count, dtype=np.float32)[:, None]
    cols = np.arange(count, dtype=np.float32)[None, :]
    angle = (np.float32(np.pi) * rows) * (cols + np.float32(0.5)) / np.float32(count)
    scale = np.where(rows == 0, np.float32(np.sqrt(1.0 / count)), np.float32(np.sqrt(2.0 / count)))
    return (scale * np.cos(angle.astype(np.float64)).astype(np.float32)).astype(np.float32)


def halves(table):
    high = table.astype(ml_dtypes.bfloat16)
    low = (table - high.astype(np.float32)).astype(ml_dtypes.bfloat16)
    return np.stack([high, low])


def split(block):
    high = block.astype(jnp.bfloat16)
    return high, (block - high.astype(jnp.float32)).astype(jnp.bfloat16)


def dot3(left, right):
    def dot(a, b):
        return jnp.dot(a, b, preferred_element_type=jnp.float32)

    return dot(left[0], right[0]) + (dot(left[0], right[1]) + dot(left[1], right[0]))


def face_stencil(diff):
    first = diff[..., 0, :]
    second = diff[..., 1, :]
    third = diff[..., 2, :]
    return jnp.stack(
        [
            WEIGHTS[0] * first + WEIGHTS[1] * second + WEIGHTS[2] * third,
            WEIGHTS[1] * first + WEIGHTS[2] * second,
            WEIGHTS[2] * first,
        ],
        axis=-2,
    )


SERIES = tuple(float((-1) ** k * 2.0 ** (2 * k + 1) / np.prod(np.arange(1.0, 2 * k + 3))) for k in range(11))


def middle(
    n_gx, n_gy, part, now, old, cx, cxt, cy, cyt, modes, cells,
    recv, mid, back, out, now_v, old_v, new_v,
    f_send, f_recv, i_send, i_recv, own_f, own_i, load, store,
):
    n = n_gx * n_gy
    planes, long_x, long_y = recv.shape
    rows_x, cols_y = part.shape[1:]
    gx = lax.axis_index("gx")
    gy = lax.axis_index("gy")
    me = gx * n_gy + gy

    def peer(k):
        other = lax.rem(me + k, n)
        return other, lax.div(other, n_gy), lax.rem(other, n_gy)

    def block(x, y):
        return (
            pl.ds(pl.multiple_of(x * rows_x, rows_x), rows_x),
            pl.ds(pl.multiple_of(y * cols_y, cols_y), cols_y),
        )

    here = block(gx, gy)

    def forward(p, k):
        other, x, y = peer(k)
        return pltpu.make_async_remote_copy(
            src_ref=part.at[other * planes + p],
            dst_ref=recv.at[(p,) + here],
            send_sem=f_send.at[p, k],
            recv_sem=f_recv.at[p, k],
            device_id={"gx": x, "gy": y},
            device_id_type=pl.DeviceIdType.MESH,
        )

    def inverse(p, k):
        other, x, y = peer(k)
        return pltpu.make_async_remote_copy(
            src_ref=out.at[(p,) + block(x, y)],
            dst_ref=cells.at[me * planes + p],
            send_sem=i_send.at[p, k],
            recv_sem=i_recv.at[p, k],
            device_id={"gx": x, "gy": y},
            device_id_type=pl.DeviceIdType.MESH,
        )

    def own_forward(p):
        return pltpu.make_async_copy(part.at[me * planes + p], recv.at[(p,) + here], own_f.at[p])

    def own_inverse(p):
        return pltpu.make_async_copy(out.at[(p,) + here], cells.at[me * planes + p], own_i.at[p])

    def start_forward(p):
        own_forward(p).start()
        for k in range(1, n):
            forward(p, k).start()

    barrier = pltpu.get_barrier_semaphore()
    for k in range(1, n):
        other, x, y = peer(k)
        pl.semaphore_signal(
            barrier, inc=1, device_id={"gx": x, "gy": y}, device_id_type=pl.DeviceIdType.MESH
        )
    pl.semaphore_wait(barrier, n - 1)

    for p in range(min(2, planes)):
        start_forward(p)
    wide = 256
    tall = 128
    for p in range(planes):
        get_now = pltpu.make_async_copy(now.at[p], now_v, load.at[0])
        get_old = pltpu.make_async_copy(old.at[p], old_v, load.at[1])
        get_now.start()
        get_old.start()
        own_forward(p).wait()
        for k in range(1, n):
            forward(p, k).wait_recv()
        if p + 2 < planes:
            start_forward(p + 2)

        @pl.loop(0, long_y // wide)
        def _(j):
            cols = pl.ds(pl.multiple_of(j * wide, wide), wide)
            mid[:, cols] = dot3((cx[0], cx[1]), split(recv[p, :, cols]))

        get_now.wait()
        get_old.wait()
        depth = n * planes
        at_z = (me * planes + p).astype(jnp.float32) / depth

        @pl.loop(0, long_x // tall)
        def _(i):
            rows = pl.ds(pl.multiple_of(i * tall, tall), tall)
            spectrum = dot3(split(mid[rows, :]), (cyt[0], cyt[1]))
            at_x = (i * tall + lax.broadcasted_iota(jnp.int32, (tall, 1), 0)).astype(
                jnp.float32
            ) / long_x
            at_y = lax.broadcasted_iota(jnp.int32, (1, long_y), 1).astype(jnp.float32) / long_y
            half = (COURANT * np.pi / 2.0) ** 2
            u = half * (at_z * at_z + at_x * at_x + at_y * at_y)
            shape = jnp.full((tall, long_y), SERIES[-1], jnp.float32)
            for term in SERIES[-2::-1]:
                shape = shape * u + term
            new = (
                (2.0 - 4.0 * (u * shape)) * now_v[rows, :]
                - old_v[rows, :]
                + (COURANT * COURANT) * shape * spectrum
            )
            new_v[rows, :] = new
            back[rows, :] = dot3(split(new), (cy[0], cy[1]))

        put = pltpu.make_async_copy(new_v, modes.at[p], store.at[0])
        put.start()

        @pl.loop(0, long_y // wide)
        def _(j):
            cols = pl.ds(pl.multiple_of(j * wide, wide), wide)
            out[p, :, cols] = dot3((cxt[0], cxt[1]), split(back[:, cols]))

        own_inverse(p).start()
        for k in range(1, n):
            inverse(p, k).start()
        put.wait()
    for p in range(planes):
        own_inverse(p).wait()
        for k in range(1, n):
            forward(p, k).wait_send()
            inverse(p, k).wait()


def through_modes(part, now, old, table_x, table_y):
    n_gx = lax.axis_size("gx")
    n_gy = lax.axis_size("gy")
    n = n_gx * n_gy
    planes, long_x, long_y = now.shape
    plane = pltpu.VMEM((long_x, long_y), jnp.float32)
    stack = pltpu.VMEM((planes, long_x, long_y), jnp.float32)
    sems = pltpu.SemaphoreType.DMA((planes, n))
    hbm = pl.BlockSpec(memory_space=pl.ANY)
    vmem = pl.BlockSpec(memory_space=pltpu.VMEM)
    return pl.pallas_call(
        functools.partial(middle, n_gx, n_gy),
        out_shape=(
            jax.ShapeDtypeStruct(now.shape, jnp.float32),
            jax.ShapeDtypeStruct(part.shape, jnp.float32),
        ),
        in_specs=[hbm] * 3 + [vmem] * 4,
        out_specs=(hbm, hbm),
        scratch_shapes=[
            stack, plane, plane, stack, plane, plane, plane,
            sems, sems, sems, sems,
            pltpu.SemaphoreType.DMA((planes,)),
            pltpu.SemaphoreType.DMA((planes,)),
            pltpu.SemaphoreType.DMA((2,)),
            pltpu.SemaphoreType.DMA((1,)),
        ],
        compiler_params=pltpu.CompilerParams(
            collective_id=0, has_side_effects=True, vmem_limit_bytes=56 * 2**20
        ),
        cost_estimate=pl.CostEstimate(
            flops=12 * planes * long_x * long_y * (long_x + long_y),
            bytes_accessed=24 * planes * long_x * long_y,
            transcendentals=0,
        ),
        name="middle",
    )(
        part,
        now,
        old,
        jnp.asarray(halves(table_x)),
        jnp.asarray(halves(table_x.T)),
        jnp.asarray(halves(table_y)),
        jnp.asarray(halves(table_y.T)),
    )


def swap(strips, devices):
    return lax.all_to_all(
        strips.reshape(devices, -1, strips.shape[1]),
        ("grp", "gx", "gy"),
        split_axis=0,
        concat_axis=0,
        tiled=True,
    ).reshape(strips.shape)


def shards(modes_now, modes_old, pressure_now, source, strip_slot, strip_row):
    depth = source.shape[1]
    rows_x = source.shape[2]
    cols_y = source.shape[3]
    long_x = modes_now.shape[2]
    long_y = modes_now.shape[3]
    table_z = jnp.asarray(cosine_table(depth))
    table_x = cosine_table(long_x)
    table_y = cosine_table(long_y)
    layers = pressure_now[0]
    top = jnp.transpose(layers[depth - 3 :][::-1], (1, 0, 2)).reshape(rows_x, 3 * cols_y)
    bottom = jnp.transpose(layers[0:3], (1, 0, 2)).reshape(rows_x, 3 * cols_y)
    devices = lax.axis_size(("grp", "gx", "gy"))
    slots_per = max(2, rows_x // devices)
    slots = strip_slot.reshape(-1)
    rows = strip_row.reshape(-1)
    places = jnp.arange(devices * slots_per, dtype=jnp.int32)
    put = (places[:, None] == slots[None, :]).astype(jnp.float32)
    label = jnp.broadcast_to((rows + 1).astype(jnp.float32)[:, None], (rows_x, 128))
    sent = jnp.dot(put, jnp.concatenate([top, label], axis=1), precision=HIGH)
    rims = swap(sent, devices)
    marks = rims[:, 3 * cols_y].astype(jnp.int32) - 1
    meet = (marks[:, None] == jnp.arange(rows_x, dtype=jnp.int32)[None, :]).astype(jnp.float32)
    met = jnp.dot(meet, bottom, precision=HIGH)
    diff = (met - rims[:, : 3 * cols_y]).reshape(-1, 3, cols_y)
    force = face_stencil(diff).reshape(-1, 3 * cols_y)
    back = swap(force, devices)
    bottom_force = -jnp.dot(meet.T, force, precision=HIGH).reshape(rows_x, 3, cols_y)
    top_force = jnp.dot(put.T, back, precision=HIGH).reshape(rows_x, 3, cols_y)
    forcing = source.at[0, 0:3].add(jnp.transpose(bottom_force, (1, 0, 2)))
    forcing = forcing.at[0, depth - 3 :].add(jnp.transpose(top_force, (1, 0, 2))[::-1])
    part = jnp.einsum("kz,zxy->kxy", table_z, forcing[0], precision=lax.Precision.HIGH)
    modes_new, cells = through_modes(part, modes_now[0], modes_old[0], table_x, table_y)
    pressure_next = jnp.einsum("kz,kxy->zxy", table_z, cells, precision=lax.Precision.HIGH)
    return (modes_new[None], pressure_next[None])


def solution(mesh):
    placed = (
        P("grp", ("gx", "gy"), None, None),
        P("grp", ("gx", "gy"), None, None),
        P("grp", None, "gx", "gy"),
        P("grp", None, "gx", "gy"),
        P("grp", "gx", "gy"),
        P("grp", "gx", "gy"),
    )
    return jax.shard_map(
        shards,
        mesh=mesh,
        in_specs=placed,
        out_specs=(P("grp", ("gx", "gy"), None, None), P("grp", None, "gx", "gy")),
        check_vma=False,
    )
```

```python
import functools

import jax
import jax.numpy as jnp
import ml_dtypes
import numpy as np
from jax import lax
from jax.experimental import pallas as pl
from jax.experimental.pallas import tpu as pltpu
from jax.sharding import PartitionSpec as P

COURANT = 0.5
WEIGHTS = (1.5, -0.15, 2.0 / 180.0)
HIGH = lax.Precision.HIGHEST


def cosine_table(count):
    rows = np.arange(count, dtype=np.float32)[:, None]
    cols = np.arange(count, dtype=np.float32)[None, :]
    angle = (np.float32(np.pi) * rows) * (cols + np.float32(0.5)) / np.float32(count)
    scale = np.where(rows == 0, np.float32(np.sqrt(1.0 / count)), np.float32(np.sqrt(2.0 / count)))
    return (scale * np.cos(angle.astype(np.float64)).astype(np.float32)).astype(np.float32)


def halves(table):
    high = table.astype(ml_dtypes.bfloat16)
    low = (table - high.astype(np.float32)).astype(ml_dtypes.bfloat16)
    return np.stack([high, low])


def split(block):
    high = block.astype(jnp.bfloat16)
    return high, (block - high.astype(jnp.float32)).astype(jnp.bfloat16)


def dot3(left, right):
    def dot(a, b):
        return jnp.dot(a, b, preferred_element_type=jnp.float32)

    return dot(left[0], right[0]) + (dot(left[0], right[1]) + dot(left[1], right[0]))


SERIES = tuple(float((-1) ** k * 2.0 ** (2 * k + 1) / np.prod(np.arange(1.0, 2 * k + 3))) for k in range(11))


def middle(
    n_gx, n_gy, part, now, old, cx, cxt, cy, cyt, modes, cells,
    recv, mid, back, out, now_v, old_v, new_v,
    f_send, f_recv, i_send, i_recv, own_f, own_i, load, store,
):
    n = n_gx * n_gy
    planes, long_x, long_y = recv.shape
    rows_x, cols_y = part.shape[1:]
    gx = lax.axis_index("gx")
    gy = lax.axis_index("gy")
    me = gx * n_gy + gy

    def peer(k):
        other = lax.rem(me + k, n)
        return other, lax.div(other, n_gy), lax.rem(other, n_gy)

    def block(x, y):
        return (
            pl.ds(pl.multiple_of(x * rows_x, rows_x), rows_x),
            pl.ds(pl.multiple_of(y * cols_y, cols_y), cols_y),
        )

    here = block(gx, gy)

    def forward(p, k):
        other, x, y = peer(k)
        return pltpu.make_async_remote_copy(
            src_ref=part.at[other * planes + p],
            dst_ref=recv.at[(p,) + here],
            send_sem=f_send.at[p, k],
            recv_sem=f_recv.at[p, k],
            device_id={"gx": x, "gy": y},
            device_id_type=pl.DeviceIdType.MESH,
        )

    def inverse(p, k):
        other, x, y = peer(k)
        return pltpu.make_async_remote_copy(
            src_ref=out.at[(p,) + block(x, y)],
            dst_ref=cells.at[me * planes + p],
            send_sem=i_send.at[p, k],
            recv_sem=i_recv.at[p, k],
            device_id={"gx": x, "gy": y},
            device_id_type=pl.DeviceIdType.MESH,
        )

    def own_forward(p):
        return pltpu.make_async_copy(part.at[me * planes + p], recv.at[(p,) + here], own_f.at[p])

    def own_inverse(p):
        return pltpu.make_async_copy(out.at[(p,) + here], cells.at[me * planes + p], own_i.at[p])

    def start_forward(p):
        own_forward(p).start()
        for k in range(1, n):
            forward(p, k).start()

    barrier = pltpu.get_barrier_semaphore()
    for k in range(1, n):
        other, x, y = peer(k)
        pl.semaphore_signal(
            barrier, inc=1, device_id={"gx": x, "gy": y}, device_id_type=pl.DeviceIdType.MESH
        )
    pl.semaphore_wait(barrier, n - 1)

    for p in range(min(2, planes)):
        start_forward(p)
    wide = 256
    tall = 128
    for p in range(planes):
        get_now = pltpu.make_async_copy(now.at[p], now_v, load.at[0])
        get_old = pltpu.make_async_copy(old.at[p], old_v, load.at[1])
        get_now.start()
        get_old.start()
        own_forward(p).wait()
        for k in range(1, n):
            forward(p, k).wait_recv()
        if p + 2 < planes:
            start_forward(p + 2)

        @pl.loop(0, long_y // wide)
        def _(j):
            cols = pl.ds(pl.multiple_of(j * wide, wide), wide)
            mid[:, cols] = dot3((cx[0], cx[1]), split(recv[p, :, cols]))

        get_now.wait()
        get_old.wait()
        depth = n * planes
        at_z = (me * planes + p).astype(jnp.float32) / depth

        @pl.loop(0, long_x // tall)
        def _(i):
            rows = pl.ds(pl.multiple_of(i * tall, tall), tall)
            spectrum = dot3(split(mid[rows, :]), (cyt[0], cyt[1]))
            at_x = (i * tall + lax.broadcasted_iota(jnp.int32, (tall, 1), 0)).astype(
                jnp.float32
            ) / long_x
            at_y = lax.broadcasted_iota(jnp.int32, (1, long_y), 1).astype(jnp.float32) / long_y
            half = (COURANT * np.pi / 2.0) ** 2
            u = half * (at_z * at_z + at_x * at_x + at_y * at_y)
            shape = jnp.full((tall, long_y), SERIES[-1], jnp.float32)
            for term in SERIES[-2::-1]:
                shape = shape * u + term
            new = (
                (2.0 - 4.0 * (u * shape)) * now_v[rows, :]
                - old_v[rows, :]
                + (COURANT * COURANT) * shape * spectrum
            )
            new_v[rows, :] = new
            back[rows, :] = dot3(split(new), (cy[0], cy[1]))

        put = pltpu.make_async_copy(new_v, modes.at[p], store.at[0])
        put.start()

        @pl.loop(0, long_y // wide)
        def _(j):
            cols = pl.ds(pl.multiple_of(j * wide, wide), wide)
            out[p, :, cols] = dot3((cxt[0], cxt[1]), split(back[:, cols]))

        own_inverse(p).start()
        for k in range(1, n):
            inverse(p, k).start()
        put.wait()
    for p in range(planes):
        own_inverse(p).wait()
        for k in range(1, n):
            forward(p, k).wait_send()
            inverse(p, k).wait()


def through_modes(part, now, old, table_x, table_y):
    n_gx = lax.axis_size("gx")
    n_gy = lax.axis_size("gy")
    n = n_gx * n_gy
    planes, long_x, long_y = now.shape
    plane = pltpu.VMEM((long_x, long_y), jnp.float32)
    stack = pltpu.VMEM((planes, long_x, long_y), jnp.float32)
    sems = pltpu.SemaphoreType.DMA((planes, n))
    hbm = pl.BlockSpec(memory_space=pl.ANY)
    vmem = pl.BlockSpec(memory_space=pltpu.VMEM)
    return pl.pallas_call(
        functools.partial(middle, n_gx, n_gy),
        out_shape=(
            jax.ShapeDtypeStruct(now.shape, jnp.float32),
            jax.ShapeDtypeStruct(part.shape, jnp.float32),
        ),
        in_specs=[hbm] * 3 + [vmem] * 4,
        out_specs=(hbm, hbm),
        scratch_shapes=[
            stack, plane, plane, stack, plane, plane, plane,
            sems, sems, sems, sems,
            pltpu.SemaphoreType.DMA((planes,)),
            pltpu.SemaphoreType.DMA((planes,)),
            pltpu.SemaphoreType.DMA((2,)),
            pltpu.SemaphoreType.DMA((1,)),
        ],
        compiler_params=pltpu.CompilerParams(
            collective_id=0, has_side_effects=True, vmem_limit_bytes=56 * 2**20
        ),
        cost_estimate=pl.CostEstimate(
            flops=12 * planes * long_x * long_y * (long_x + long_y),
            bytes_accessed=24 * planes * long_x * long_y,
            transcendentals=0,
        ),
        name="middle",
    )(
        part,
        now,
        old,
        jnp.asarray(halves(table_x)),
        jnp.asarray(halves(table_x.T)),
        jnp.asarray(halves(table_y)),
        jnp.asarray(halves(table_y.T)),
    )


def analyse(layers, table):
    count = len(layers)
    if count == 1:
        return [layers[0] * float(table[0, 0])]
    mid = count // 2
    sums = [layers[m] + layers[count - 1 - m] for m in range(mid)]
    gaps = [layers[m] - layers[count - 1 - m] for m in range(mid)]
    modes = [None] * count
    for k in range(1, count, 2):
        total = gaps[0] * float(table[k, 0])
        for m in range(1, mid):
            total = total + gaps[m] * float(table[k, m])
        modes[k] = total
    modes[0::2] = analyse(sums, table[0::2, :mid])
    return modes


def synthesise(modes, table):
    count = len(modes)
    if count == 1:
        return [modes[0] * float(table[0, 0])]
    mid = count // 2
    even = synthesise(modes[0::2], table[0::2, :mid])
    layers = [None] * count
    for m in range(mid):
        odd = modes[1] * float(table[1, m])
        for k in range(3, count, 2):
            odd = odd + modes[k] * float(table[k, m])
        layers[m] = even[m] + odd
        layers[count - 1 - m] = even[m] - odd
    return layers


def tiles(ref, body):
    rows, cols = ref.shape[1:]
    across = cols // 128

    @pl.loop(0, (rows // 8) * across)
    def _(t):
        row = pl.multiple_of(lax.div(t, across) * 8, 8)
        col = pl.multiple_of(lax.rem(t, across) * 128, 128)
        body(pl.ds(row, 8), col)


def depth_in(table, source, low, high, part):
    depth, _, cols_y = source.shape

    def body(rows, col):
        layers = [source[z, rows, pl.ds(col, 128)] for z in range(depth)]
        for j in range(3):
            at = pl.ds(pl.multiple_of(j * cols_y + col, 128), 128)
            layers[j] = layers[j] - low[rows, at]
            layers[depth - 1 - j] = layers[depth - 1 - j] + high[rows, at]
        for k, mode in enumerate(analyse(layers, table)):
            part[k, rows, pl.ds(col, 128)] = mode

    tiles(source, body)


def depth_out(table, cells, field):
    depth = cells.shape[0]

    def body(rows, col):
        modes = [cells[k, rows, pl.ds(col, 128)] for k in range(depth)]
        for z, layer in enumerate(synthesise(modes, table)):
            field[z, rows, pl.ds(col, 128)] = layer

    tiles(cells, body)


def over_depth(body, table, field, *strips):
    depth, rows_x, cols_y = field.shape
    rows = 16
    block = pl.BlockSpec((depth, rows, cols_y), lambda i: (0, i, 0))
    strip = pl.BlockSpec((rows, 3 * cols_y), lambda i: (i, 0))
    return pl.pallas_call(
        functools.partial(body, table),
        grid=(rows_x // rows,),
        out_shape=jax.ShapeDtypeStruct(field.shape, jnp.float32),
        in_specs=[block] + [strip] * len(strips),
        out_specs=block,
        compiler_params=pltpu.CompilerParams(vmem_limit_bytes=24 * 2**20),
    )(field, *strips)


def lay_faces(low0, low1, low2, high0, high1, high2, bottom, top):
    cols_y = low0.shape[2]
    for j, (low, high) in enumerate(((low0, high0), (low1, high1), (low2, high2))):
        bottom[:, j * cols_y : (j + 1) * cols_y] = low[0]
        top[:, j * cols_y : (j + 1) * cols_y] = high[0]


def faces(pressure):
    depth, rows_x, cols_y = pressure.shape

    def layer(z):
        return pl.BlockSpec((1, rows_x, cols_y), lambda i: (z, 0, 0))

    flat = jax.ShapeDtypeStruct((rows_x, 3 * cols_y), jnp.float32)
    whole = pl.BlockSpec((rows_x, 3 * cols_y), lambda i: (0, 0))
    return pl.pallas_call(
        lay_faces,
        grid=(1,),
        out_shape=(flat, flat),
        in_specs=[layer(z) for z in (0, 1, 2, depth - 1, depth - 2, depth - 3)],
        out_specs=(whole, whole),
        compiler_params=pltpu.CompilerParams(vmem_limit_bytes=24 * 2**20),
    )(*[pressure] * 6)


def swap(strips, devices):
    return lax.all_to_all(
        strips.reshape(devices, -1, strips.shape[1]),
        ("grp", "gx", "gy"),
        split_axis=0,
        concat_axis=0,
        tiled=True,
    ).reshape(strips.shape)


def shards(modes_now, modes_old, pressure_now, source, strip_slot, strip_row):
    depth = source.shape[1]
    rows_x = source.shape[2]
    cols_y = source.shape[3]
    long_x = modes_now.shape[2]
    long_y = modes_now.shape[3]
    table_z = cosine_table(depth)
    table_x = cosine_table(long_x)
    table_y = cosine_table(long_y)
    bottom, top = faces(pressure_now[0])
    devices = lax.axis_size(("grp", "gx", "gy"))
    slots_per = max(2, rows_x // devices)
    slots = strip_slot.reshape(-1)
    rows = strip_row.reshape(-1)
    places = jnp.arange(devices * slots_per, dtype=jnp.int32)
    put = (places[:, None] == slots[None, :]).astype(jnp.float32)
    label = jnp.broadcast_to((rows + 1).astype(jnp.float32)[:, None], (rows_x, 128))
    sent = jnp.dot(put, jnp.concatenate([top, label], axis=1), precision=HIGH)
    rims = swap(sent, devices)
    marks = rims[:, 3 * cols_y].astype(jnp.int32) - 1
    meet = (marks[:, None] == jnp.arange(rows_x, dtype=jnp.int32)[None, :]).astype(jnp.float32)
    met = jnp.dot(meet, bottom, precision=HIGH)
    diff = met - rims[:, : 3 * cols_y]
    first, second, third = (diff[:, j * cols_y : (j + 1) * cols_y] for j in range(3))
    force = jnp.concatenate(
        [
            WEIGHTS[0] * first + WEIGHTS[1] * second + WEIGHTS[2] * third,
            WEIGHTS[1] * first + WEIGHTS[2] * second,
            WEIGHTS[2] * first,
        ],
        axis=1,
    )
    back = swap(force, devices)
    bottom_force = jnp.dot(meet.T, force, precision=HIGH)
    top_force = jnp.dot(put.T, back, precision=HIGH)
    part = over_depth(depth_in, table_z, source[0], bottom_force, top_force)
    modes_new, cells = through_modes(part, modes_now[0], modes_old[0], table_x, table_y)
    pressure_next = over_depth(depth_out, table_z, cells)
    return (modes_new[None], pressure_next[None])


def solution(mesh):
    placed = (
        P("grp", ("gx", "gy"), None, None),
        P("grp", ("gx", "gy"), None, None),
        P("grp", None, "gx", "gy"),
        P("grp", None, "gx", "gy"),
        P("grp", "gx", "gy"),
        P("grp", "gx", "gy"),
    )
    return jax.shard_map(
        shards,
        mesh=mesh,
        in_specs=placed,
        out_specs=(P("grp", ("gx", "gy"), None, None), P("grp", None, "gx", "gy")),
        check_vma=False,
    )
```
